32 devices in a mesh: row: 8 (over z, y), col: 4 (over x, core).
Axes of the slice: x: 2, y: 2, z: 4, core: 2. Of those that a mesh axis runs over, the one named last changes fastest.
Arguments:
- roll_embed: bfloat16 [512, 3072], P('col', 'row'), may hold values from -16 to 16
- expert_embed: bfloat16 [512, 8192], P('row', 'col'), may hold values from -16 to 16
- roll_weight: float32 [3072], P('row'), may hold values from 0.5 to 2
- expert_weight: float32 [8192], P('col'), may hold values from 0.5 to 2
Outputs:
- reward: float32 [3072], P('row')
- roll_pull: float32 [512, 3072], P('col', 'row')
- expert_pull: float32 [512, 8192], P('row', 'col')
The draws below stay inside these ranges and needn't reach their ends.
All inputs are finite; a program needn't handle non-finite values.
Results may differ from the reference program's by a relative error of at most 0.0022.
Values may be sent and summed in bfloat16 or wider, within the bound.
A program may use at most 64 MiB of HBM per device.

```python
import math
import jax
import jax.numpy as jnp
from jax import lax

EMB = 512
ITERS = 3
NR = 3072
NE = 8192


def embed_draw(key, rows, cols):
    first = jax.random.fold_in(key, 11)
    values = jax.random.normal(first, (rows, cols), jnp.float32)
    return jnp.clip(values, -16.0, 16.0).astype(jnp.bfloat16)


def draw_roll_embed(key, part):
    return embed_draw(key, EMB, NR)


def draw_expert_embed(key, part):
    return embed_draw(key, EMB, NE)


def steps_of(rng, shape, cuts, low, largest):
    level = 1.0
    for dim, shards_of in cuts:
        steps = jax.random.uniform(jax.random.fold_in(jax.random.fold_in(rng, 6), dim), (shards_of,), jnp.float32, low / len(cuts), largest / len(cuts))
        level = level * jnp.repeat(jnp.exp(steps), shape[dim] // shards_of).reshape((-1,) + (1,) * (len(shape) - 1 - dim))
    return level


def setup_inputs(seed: int = 0) -> dict:
    arg_keys = jax.random.split(jax.random.key(seed), 5)
    roll_embed = draw_roll_embed(jax.random.fold_in(arg_keys[4], 71), 0)
    expert_embed = draw_expert_embed(jax.random.fold_in(arg_keys[4], 71), 0)
    roll_weight = jnp.clip(jnp.exp(math.log(2.0) - 1.3862944 * jax.random.uniform(arg_keys[2], (NR,), jnp.float32) ** steps_of(arg_keys[2], (NR,), ((0, 8),), -0.2, 0.2)), 0.5, 2.0)
    expert_weight = jnp.clip(jnp.exp(math.log(2.0) - 1.3862944 * jax.random.uniform(arg_keys[3], (NE,), jnp.float32) ** steps_of(arg_keys[3], (NE,), ((0, 4),), -0.2, 0.2)), 0.5, 2.0)
    return {"roll_embed": roll_embed, "expert_embed": expert_embed, "roll_weight": roll_weight, "expert_weight": expert_weight}


blur = 0.05


def cost_rows(xb, yf, sqx_b, sqy):
    cross = jnp.dot(xb.T, yf, precision=lax.Precision.HIGHEST)
    return (sqx_b[:, None] + sqy[None, :] - 2.0 * cross) / EMB


def reference(roll_embed, expert_embed, roll_weight, expert_weight):
    xf = roll_embed.astype(jnp.float32)
    yf = expert_embed.astype(jnp.float32)
    sqx = jnp.sum(xf * xf, 0)
    sqy = jnp.sum(yf * yf, 0)
    log_a = blur * jnp.log(roll_weight)
    log_b = blur * jnp.log(expert_weight)
    block = min(256, NR)
    nblocks = NR // block
    starts = jnp.arange(nblocks, dtype=jnp.int32) * block

    def rows_of(start):
        xb = lax.dynamic_slice_in_dim(xf, start, block, 1)
        sb = lax.dynamic_slice_in_dim(sqx, start, block, 0)
        return xb, cost_rows(xb, yf, sb, sqy)

    def row_lse(gvals):
        def one(start):
            xb, cost = rows_of(start)
            score = (gvals[None, :] - cost) / blur
            top = jnp.max(score, 1)
            return top + jnp.log(jnp.sum(jnp.exp(score - top[:, None]), 1))
        return lax.map(one, starts).reshape(NR)

    def col_lse(fvals):
        def step(carry, start):
            xb, cost = rows_of(start)
            fb = lax.dynamic_slice_in_dim(fvals, start, block, 0)
            score = (fb[:, None] - cost) / blur
            top = jnp.max(score, 0)
            total = jnp.sum(jnp.exp(score - top[None, :]), 0)
            high = jnp.maximum(carry[0], top)
            merged = carry[1] * jnp.exp(carry[0] - high) + total * jnp.exp(top - high)
            return (high, merged), None
        init = (jnp.full((NE,), -1e30, jnp.float32), jnp.zeros((NE,), jnp.float32))
        (top, total), _ = lax.scan(step, init, starts)
        return top + jnp.log(total)

    fvals = jnp.zeros((NR,), jnp.float32)
    gvals = jnp.zeros((NE,), jnp.float32)
    for step_index in range(ITERS):
        fvals = log_a - blur * row_lse(gvals)
        gvals = log_b - blur * col_lse(fvals)

    def final(carry, start):
        xb, cost = rows_of(start)
        fb = lax.dynamic_slice_in_dim(fvals, start, block, 0)
        plan = jnp.exp((fb[:, None] + gvals[None, :] - cost) / blur)
        rowmass = jnp.sum(plan, 1)
        score = (gvals[None, :] - cost) / blur
        top = jnp.max(score, 1)
        shifted = jnp.exp(score - top[:, None])
        reward_b = -jnp.sum(shifted * cost, 1) / jnp.sum(shifted, 1)
        plan_bf = plan.astype(jnp.bfloat16).astype(jnp.float32)
        pulled = jnp.dot(yf, plan_bf.T, precision=lax.Precision.HIGHEST)
        carry = carry + jnp.dot(xb, plan_bf, precision=lax.Precision.HIGHEST)
        return carry, (rowmass, reward_b, pulled)

    xsum, (rowmass, reward, pulled) = lax.scan(final, jnp.zeros((EMB, NE), jnp.float32), starts)
    rowmass = rowmass.reshape(NR)
    reward = reward.reshape(NR)
    pulled = jnp.transpose(pulled, (1, 0, 2)).reshape(EMB, NR)
    roll_pull = rowmass[None, :] * xf - pulled
    expert_pull = expert_weight[None, :] * yf - xsum
    return reward, roll_pull, expert_pull
```

```python
import functools
import math

import jax
import jax.numpy as jnp
from jax import lax
from jax.experimental import pallas as pl
from jax.experimental.pallas import tpu as pltpu
from jax.sharding import PartitionSpec as P

ITERS = 3


blur = 0.05

LANES = 128
LOG2E = math.log2(math.e)
MESH = pl.DeviceIdType.MESH


def lse2(parts):
    top = jnp.max(parts, 0)
    return top + jnp.log(jnp.sum(jnp.exp2(parts - top[None]), 0)) * LOG2E


def tile_rows(blocks):
    return -(-blocks // 8) * 8


def kernel(
    zn, yn, cn, x_ref, y_ref, a_ref, b_ref,
    reward_ref, mass_ref, pulled_ref, xsum_ref,
    xg, yg, neg, plan, fbc, logw, fslots, gslots, rslots, fv, gv,
    xsend, xrecv, psend, precv,
    local_sem, xs, xr, ys, yr, ws, wr, fs, fr, gs, gr, rs, rr, us, ur, ps, pr,
):
    row, col = lax.axis_index("row"), lax.axis_index("col")
    z, y = lax.div(row, yn), lax.rem(row, yn)
    nrow, ncube = zn * yn, cn * yn
    q = col * yn + y
    fx, own_rows = x_ref.shape
    fy = y_ref.shape[0]
    width, rows = xg.shape
    cols = yg.shape[1]
    rblocks, cblocks = rows // LANES, cols // LANES

    def cube_device(index):
        return (z * yn + lax.rem(index, yn), lax.div(index, yn))

    def each(count, body):
        def step(i, carry):
            body(i)
            return carry
        lax.fori_loop(0, count, step, 0)

    def others(count, me, body):
        each(count - 1, lambda i: body(lax.rem(me + i + 1, count)))

    def band(index, size):
        return pl.ds(pl.multiple_of(index * size, size), size)

    fslots[...] = jnp.zeros(fslots.shape, jnp.float32)
    gslots[...] = jnp.zeros(gslots.shape, jnp.float32)
    rslots[...] = jnp.zeros(rslots.shape, jnp.float32)
    barrier = pltpu.get_barrier_semaphore()
    others(nrow, row, lambda r: pl.semaphore_signal(
        barrier, inc=1, device_id=(r, col), device_id_type=MESH))
    others(ncube, q, lambda p: pl.semaphore_signal(
        barrier, inc=1, device_id=cube_device(p), device_id_type=MESH))
    pl.semaphore_wait(barrier, nrow - 1 + ncube - 1)

    def y_copy(dest, origin):
        return pltpu.make_async_remote_copy(
            src_ref=y_ref.at[:, band(lax.rem(dest, yn), cols)],
            dst_ref=yg.at[band(origin, fy), :],
            send_sem=ys.at[dest], recv_sem=yr.at[origin],
            device_id=(dest, col), device_id_type=MESH)

    def x_copy(dest, origin):
        return pltpu.make_async_remote_copy(
            src_ref=x_ref,
            dst_ref=xg.at[band(lax.div(origin, yn), fx), band(lax.rem(origin, yn), own_rows)],
            send_sem=xs.at[dest], recv_sem=xr.at[origin],
            device_id=cube_device(dest), device_id_type=MESH)

    def w_copy(dest, origin):
        return pltpu.make_async_remote_copy(
            src_ref=logw.at[origin], dst_ref=logw.at[origin],
            send_sem=ws.at[dest], recv_sem=wr.at[origin],
            device_id=(z * yn + dest, col), device_id_type=MESH)

    others(nrow, row, lambda r: y_copy(r, row).start())
    others(ncube, q, lambda p: x_copy(p, q).start())
    own_blocks = own_rows // LANES
    logw[y] = jnp.zeros(logw.shape[1:], jnp.float32)
    logw[y, 0:own_blocks, :] = jnp.log(a_ref[...]) * LOG2E
    others(yn, y, lambda p: w_copy(p, y).start())
    own_y = pltpu.make_async_copy(
        y_ref.at[:, band(y, cols)], yg.at[band(row, fy), :], local_sem.at[0])
    own_x = pltpu.make_async_copy(
        x_ref, xg.at[band(col, fx), band(y, own_rows)], local_sem.at[1])
    own_y.start()
    own_x.start()
    fv[...] = jnp.zeros(fv.shape, jnp.float32)
    gv[...] = jnp.zeros(gv.shape, jnp.float32)
    log_b = jnp.log(b_ref[y]) * LOG2E
    own_y.wait()
    own_x.wait()
    others(yn, y, lambda p: w_copy(p, p).wait_recv())
    others(ncube, q, lambda p: x_copy(p, p).wait_recv())

    def spread(line):
        return jnp.transpose(jnp.broadcast_to(line, (LANES, LANES)))

    def gather_line(column):
        return jnp.transpose(jnp.broadcast_to(column, (LANES, LANES)))[0:1, :]

    log_a = jnp.concatenate([logw[p, 0:own_blocks, :] for p in range(yn)], 0)
    others(nrow, row, lambda r: y_copy(r, r).wait_recv())

    scale = LOG2E / (blur * width)
    yall = yg[...].astype(jnp.float32)
    sqy = jnp.sum(yall * yall, 0, keepdims=True)

    def cost_block(i):
        xb = xg[:, band(i, LANES)]
        xf = xb.astype(jnp.float32)
        sqx = spread(jnp.sum(xf * xf, 0, keepdims=True))[:, 0:1]
        cross = lax.dot_general(
            xb, yg[...], (((0,), (0,)), ((), ())), preferred_element_type=jnp.float32)
        neg[band(i, LANES), :] = (2.0 * cross - (sqx + sqy)) * scale
    each(rblocks, cost_block)

    def row_block(i):
        here = band(i, LANES)

        def score(k):
            return neg[here, k * LANES:(k + 1) * LANES] + gv[k:k + 1, :]

        high = score(0)
        for k in range(1, cblocks):
            high = jnp.maximum(high, score(k))
        top = jnp.max(high, 1, keepdims=True)
        return here, score, top

    def finish(top, total):
        return top + jnp.log(jnp.sum(total, 1, keepdims=True)) * LOG2E

    def exchange(slots, count, me, sends, recvs, device):
        def copy(dest, origin):
            return pltpu.make_async_remote_copy(
                src_ref=slots.at[origin], dst_ref=slots.at[origin],
                send_sem=sends.at[dest], recv_sem=recvs.at[origin],
                device_id=device(dest), device_id_type=MESH)
        others(count, me, lambda p: copy(p, me).start())

        def arrive():
            others(count, me, lambda p: copy(p, p).wait_recv())

        def leave():
            others(count, me, lambda p: copy(p, me).wait_send())
        return arrive, leave

    leaves = []
    for t in range(ITERS):
        def row_pass(i):
            here, score, top = row_block(i)
            total = jnp.exp2(score(0) - top)
            for k in range(1, cblocks):
                total = total + jnp.exp2(score(k) - top)
            fslots[t, q, pl.ds(i, 1), :] = gather_line(finish(top, total))
        each(rblocks, row_pass)
        arrive, leave = exchange(fslots.at[t], ncube, q, fs.at[t], fr.at[t], cube_device)
        leaves.append(leave)
        arrive()
        fv[0:rblocks, :] = log_a - lse2(fslots[t, :, 0:rblocks, :])
        for i in range(rblocks):
            fbc[i * LANES:(i + 1) * LANES, :] = spread(fv[i:i + 1, :])

        def col_pass(k):
            here = band(k, LANES)

            def score(i):
                part = slice(i * LANES, (i + 1) * LANES)
                return neg[part, here] + fbc[part, :]

            high = score(0)
            for i in range(1, rblocks):
                high = jnp.maximum(high, score(i))
            top = jnp.max(high, 0, keepdims=True)
            total = jnp.exp2(score(0) - top)
            for i in range(1, rblocks):
                total = total + jnp.exp2(score(i) - top)
            line = top + jnp.log(jnp.sum(total, 0, keepdims=True)) * LOG2E
            gslots[t, z, pl.ds(k, 1), :] = line
        each(cblocks, col_pass)
        arrive, leave = exchange(
            gslots.at[t], zn, z, gs.at[t], gr.at[t], lambda p: (p * yn + y, col))
        leaves.append(leave)
        arrive()
        gv[0:cblocks, :] = log_b - lse2(gslots[t, :, 0:cblocks, :])

    def plan_block(i):
        here = band(i, LANES)
        for k in range(cblocks):
            part = slice(k * LANES, (k + 1) * LANES)
            value = jnp.exp2(neg[here, part] + fbc[here, :] + gv[k:k + 1, :])
            plan[here, part] = value.astype(jnp.bfloat16)
    each(rblocks, plan_block)

    step = 2 * LANES if cols % (2 * LANES) == 0 else LANES

    def xsum_block(k):
        here = band(k, step)
        xsend[:, here] = jnp.dot(
            xg[...], plan[:, here], preferred_element_type=jnp.float32).astype(jnp.bfloat16)
    each(cols // step, xsum_block)

    def u_copy(dest, origin):
        return pltpu.make_async_remote_copy(
            src_ref=xsend.at[band(dest, fy), :], dst_ref=xrecv.at[origin],
            send_sem=us.at[dest], recv_sem=ur.at[origin],
            device_id=(dest, col), device_id_type=MESH)
    others(nrow, row, lambda r: u_copy(r, row).start())
    own_u = pltpu.make_async_copy(xsend.at[band(row, fy), :], xrecv.at[row], local_sem.at[0])
    own_u.start()

    rstep = 2 * LANES if rows % (2 * LANES) == 0 else LANES

    def pull_block(i):
        here = band(i, rstep)
        psend[:, here] = lax.dot_general(
            yg[...], plan[here, :], (((1,), (1,)), ((), ())),
            preferred_element_type=jnp.float32).astype(jnp.bfloat16)
    each(rows // rstep, pull_block)

    def p_source(dest):
        return psend.at[band(lax.div(dest, yn), fx), band(lax.rem(dest, yn), own_rows)]

    def p_copy(dest, origin):
        return pltpu.make_async_remote_copy(
            src_ref=p_source(dest), dst_ref=precv.at[origin],
            send_sem=ps.at[dest], recv_sem=pr.at[origin],
            device_id=cube_device(dest), device_id_type=MESH)
    others(ncube, q, lambda p: p_copy(p, q).start())
    own_p = pltpu.make_async_copy(p_source(q), precv.at[q], local_sem.at[1])
    own_p.start()

    half = rslots.shape[1] // 2

    def reward_pass(i):
        here, score, top = row_block(i)
        total = jnp.zeros((LANES, LANES), jnp.float32)
        moment = jnp.zeros((LANES, LANES), jnp.float32)
        for k in range(cblocks):
            weight = jnp.exp2(score(k) - top)
            total = total + weight
            moment = moment + weight * neg[here, k * LANES:(k + 1) * LANES]
        mean = jnp.sum(moment, 1, keepdims=True) / jnp.sum(total, 1, keepdims=True)
        rslots[q, pl.ds(i, 1), :] = gather_line(finish(top, total))
        rslots[q, pl.ds(half + i, 1), :] = gather_line(mean)
    each(rblocks, reward_pass)
    arrive, leave = exchange(rslots, ncube, q, rs, rr, cube_device)
    leaves.append(leave)
    arrive()
    logs = rslots[:, 0:rblocks, :]
    top = jnp.max(logs, 0)
    share = jnp.exp2(logs - top[None])
    total = jnp.sum(share, 0)
    mean = jnp.sum(share * rslots[:, half:half + rblocks, :], 0) / total
    reward_ref[...] = mean * (blur / LOG2E)
    mass_ref[...] = jnp.exp2(fv[0:rblocks, :] + top) * total

    own_p.wait()
    others(ncube, q, lambda p: p_copy(p, p).wait_recv())
    summed = precv[0].astype(jnp.float32)
    for p in range(1, ncube):
        summed = summed + precv[p].astype(jnp.float32)
    pulled_ref[...] = summed
    own_u.wait()
    others(nrow, row, lambda r: u_copy(r, r).wait_recv())
    for p in range(yn):
        summed = xrecv[p].astype(jnp.float32)
        for s in range(1, zn):
            summed = summed + xrecv[s * yn + p].astype(jnp.float32)
        xsum_ref[:, p * cols:(p + 1) * cols] = summed

    others(nrow, row, lambda r: y_copy(r, row).wait_send())
    others(ncube, q, lambda p: x_copy(p, q).wait_send())
    others(yn, y, lambda p: w_copy(p, y).wait_send())
    for leave in leaves:
        leave()
    others(nrow, row, lambda r: u_copy(r, row).wait_send())
    others(ncube, q, lambda p: p_copy(p, q).wait_send())


def shards(zn, yn, cn, roll_embed, expert_embed, roll_weight, expert_weight):
    fx, own_rows = roll_embed.shape
    fy, own_cols = expert_embed.shape
    width = fx * cn
    rows, cols = own_rows * yn, own_cols // yn
    rblocks, cblocks = rows // LANES, cols // LANES
    nrow, ncube = zn * yn, cn * yn
    f32, bf16 = jnp.float32, jnp.bfloat16
    dma = pltpu.SemaphoreType.DMA
    rt, ct, wt = tile_rows(rblocks), tile_rows(cblocks), tile_rows(own_rows // LANES)
    vmem = pl.BlockSpec(memory_space=pltpu.VMEM)
    reward, mass, pulled, xsum = pl.pallas_call(
        functools.partial(kernel, zn, yn, cn),
        out_shape=(
            jax.ShapeDtypeStruct((rblocks, LANES), f32),
            jax.ShapeDtypeStruct((rblocks, LANES), f32),
            jax.ShapeDtypeStruct((fx, own_rows), f32),
            jax.ShapeDtypeStruct((fy, own_cols), f32),
        ),
        in_specs=[vmem] * 4,
        out_specs=[vmem] * 4,
        scratch_shapes=[
            pltpu.VMEM((width, rows), bf16),
            pltpu.VMEM((width, cols), bf16),
            pltpu.VMEM((rows, cols), f32),
            pltpu.VMEM((rows, cols), bf16),
            pltpu.VMEM((rows, LANES), f32),
            pltpu.VMEM((yn, wt, LANES), f32),
            pltpu.VMEM((ITERS, ncube, rt, LANES), f32),
            pltpu.VMEM((ITERS, zn, ct, LANES), f32),
            pltpu.VMEM((ncube, 2 * rt, LANES), f32),
            pltpu.VMEM((rt, LANES), f32),
            pltpu.VMEM((ct, LANES), f32),
            pltpu.VMEM((width, cols), bf16),
            pltpu.VMEM((nrow, fy, cols), bf16),
            pltpu.VMEM((width, rows), bf16),
            pltpu.VMEM((ncube, fx, own_rows), bf16),
            dma((2,)),
            dma((ncube,)), dma((ncube,)),
            dma((nrow,)), dma((nrow,)),
            dma((yn,)), dma((yn,)),
            dma((ITERS, ncube)), dma((ITERS, ncube)),
            dma((ITERS, zn)), dma((ITERS, zn)),
            dma((ncube,)), dma((ncube,)),
            dma((nrow,)), dma((nrow,)),
            dma((ncube,)), dma((ncube,)),
        ],
        compiler_params=pltpu.CompilerParams(
            collective_id=0, has_side_effects=True, vmem_limit_bytes=40 * 2**20),
        cost_estimate=pl.CostEstimate(
            flops=6 * rows * cols * width, bytes_accessed=4 * fy * own_cols,
            transcendentals=8 * rows * cols),
    )(
        roll_embed, expert_embed,
        roll_weight.reshape(own_rows // LANES, LANES),
        expert_weight.reshape(yn, cblocks, LANES),
    )
    start = lax.rem(lax.axis_index("row"), yn) * own_rows
    reward = lax.dynamic_slice_in_dim(reward.reshape(rows), start, own_rows, 0)
    mass = lax.dynamic_slice_in_dim(mass.reshape(rows), start, own_rows, 0)
    roll_pull = mass[None, :] * roll_embed.astype(f32) - pulled
    expert_pull = expert_weight[None, :] * expert_embed.astype(f32) - xsum
    return (reward, roll_pull, expert_pull)


def solution(mesh):
    cn = mesh.shape["col"]
    yn = max(cn // 2, 1)
    if mesh.shape["row"] % yn:
        yn = 1
    zn = mesh.shape["row"] // yn
    placed = (P("col", "row"), P("row", "col"), P("row"), P("col"))
    return jax.shard_map(
        functools.partial(shards, zn, yn, cn),
        mesh=mesh,
        in_specs=placed,
        out_specs=(P("row"), P("col", "row"), P("row", "col")),
        check_vma=False,
    )
```

```python
import functools
import math

import jax
import jax.numpy as jnp
from jax import lax
from jax.experimental import pallas as pl
from jax.experimental.pallas import tpu as pltpu
from jax.sharding import PartitionSpec as P

ITERS = 3


blur = 0.05

LANES = 128
LOG2E = math.log2(math.e)
MESH = pl.DeviceIdType.MESH


def lse2(parts):
    top = jnp.max(parts, 0)
    return top + jnp.log(jnp.sum(jnp.exp2(parts - top[None]), 0)) * LOG2E


def tile_rows(blocks):
    return -(-blocks // 8) * 8


def kernel(
    zn, yn, cn, split, x_ref, y_ref, a_ref, b_ref,
    reward_ref, mass_ref, pulled_ref, xsum_ref,
    xg, yg, neg, pm, plan, fbc, wslots, fslots, gslots, rslots, fv, gv,
    xsend, xmid, xout, xrecv, psend, pmid, pout, precv,
    local_sem, xs, xr, xf, ys, yr, yf, ws, wr, fs, fr, gs, gr, rs, rr,
    us, um, uo, ur, ps, pk, po, pr,
):
    row, col = lax.axis_index("row"), lax.axis_index("col")
    z, y = lax.div(row, yn), lax.rem(row, yn)
    zh, zl = lax.div(z, split), lax.rem(z, split)
    cores = 2 if cn % 2 == 0 else 1
    c = lax.rem(col, cores)
    nrow, ncube, nside = zn * yn, cn * split, (zn // split) * yn
    nchip = ncube // cores
    q = col * split + zl
    chip = lax.div(col, cores) * split + zl
    side = zh * yn + y
    fx, own_rows = x_ref.shape
    fy = y_ref.shape[0]
    width, rows = xg.shape
    cols = yg.shape[1]
    rblocks, cblocks = rows // LANES, cols // LANES
    own_blocks = own_rows // LANES

    def cube_device(index):
        return ((zh * split + lax.rem(index, split)) * yn + y, lax.div(index, split))

    def side_device(index):
        peer = lax.div(index, yn) * split + zl
        return (peer * yn + lax.rem(index, yn), col)

    def cube_index(index, core):
        return (lax.div(index, split) * cores + core) * split + lax.rem(index, split)

    def each(count, body):
        def step(i, carry):
            body(i)
            return carry
        if count > 0:
            lax.fori_loop(0, count, step, 0)

    def others(count, me, body):
        each(count - 1, lambda i: body(lax.rem(me + i + 1, count)))

    def band(index, size):
        return pl.ds(pl.multiple_of(index * size, size), size)

    def remote(src, dst, send, recv, device):
        return pltpu.make_async_remote_copy(
            src_ref=src, dst_ref=dst, send_sem=send, recv_sem=recv,
            device_id=device, device_id_type=MESH)

    wslots[...] = jnp.ones(wslots.shape, jnp.float32)
    wslots[zl, 0:own_blocks, :] = a_ref[...]
    fslots[...] = jnp.zeros(fslots.shape, jnp.float32)
    gslots[...] = jnp.zeros(gslots.shape, jnp.float32)
    rslots[...] = jnp.zeros(rslots.shape, jnp.float32)
    barrier = pltpu.get_barrier_semaphore()
    others(nrow, row, lambda r: pl.semaphore_signal(
        barrier, inc=1, device_id=(r, col), device_id_type=MESH))
    others(ncube, q, lambda p: pl.semaphore_signal(
        barrier, inc=1, device_id=cube_device(p), device_id_type=MESH))
    pl.semaphore_wait(barrier, nrow - 1 + ncube - 1)

    def y_place(origin):
        return yg.at[band(origin, fy), :]

    def y_along(dest, origin):
        return remote(
            y_ref.at[:, band(lax.rem(dest, split), cols)], y_place(origin * yn + y),
            ys.at[dest], yr.at[origin * yn + y], (dest * yn + y, col))

    def y_across(layer, dest, origin):
        place = y_place(layer * yn + origin)
        return remote(
            place, place, yf.at[layer, dest], yr.at[layer * yn + origin], (z * yn + dest, col))

    def y_first(dest):
        return remote(
            y_ref.at[:, band(zl, cols)], y_place(row), yf.at[z, dest], yr.at[row],
            (z * yn + dest, col))

    def x_place(index):
        return xg.at[band(lax.div(index, split), fx), band(lax.rem(index, split), own_rows)]

    def x_copy(dest, origin):
        return remote(x_ref, x_place(origin), xs.at[dest], xr.at[origin], cube_device(dest))

    def x_forward(origin, core):
        return remote(
            x_place(origin), x_place(origin), xf.at[origin, core], xr.at[origin],
            cube_device(cube_index(chip, core)))

    def w_copy(dest, origin):
        return remote(
            wslots.at[origin], wslots.at[origin], ws.at[dest], wr.at[origin],
            ((zh * split + dest) * yn + y, col))

    others(zn, z, lambda p: y_along(p, z).start())
    others(yn, y, lambda p: y_first(p).start())
    others(nchip, chip, lambda p: x_copy(cube_index(p, c), q).start())
    others(cores, c, lambda p: x_copy(cube_index(chip, p), q).start())
    others(split, zl, lambda p: w_copy(p, zl).start())
    own_y = pltpu.make_async_copy(y_ref.at[:, band(zl, cols)], y_place(row), local_sem.at[0])
    own_x = pltpu.make_async_copy(x_ref, x_place(q), local_sem.at[1])
    own_y.start()
    own_x.start()

    def x_relay(p):
        origin = cube_index(p, c)
        x_copy(origin, origin).wait_recv()
        others(cores, c, lambda core: x_forward(origin, core).start())
    others(nchip, chip, x_relay)

    def y_relay(p):
        y_along(p, p).wait_recv()
        others(yn, y, lambda dest: y_across(p, dest, y).start())
    others(zn, z, y_relay)

    log_b = jnp.log(b_ref[zl]) * LOG2E
    own_y.wait()
    own_x.wait()
    others(split, zl, lambda p: w_copy(p, p).wait_recv())
    mass_a = jnp.concatenate([wslots[p, 0:own_blocks, :] for p in range(split)], 0)
    log_a = jnp.log(mass_a) * LOG2E

    def x_rest(core):
        each(nchip, lambda p: x_copy(cube_index(p, core), cube_index(p, core)).wait_recv())
    others(cores, c, x_rest)

    def y_rest(p):
        each(zn, lambda layer: y_across(layer, p, p).wait_recv())
    others(yn, y, y_rest)

    def spread(line):
        return jnp.transpose(jnp.broadcast_to(line, (LANES, LANES)))

    def gather_line(column):
        return jnp.transpose(jnp.broadcast_to(column, (LANES, LANES)))[0:1, :]

    def row_sums(block):
        return jnp.sum(jnp.transpose(block), 0, keepdims=True)

    def part(index):
        return slice(index * LANES, (index + 1) * LANES)

    scale = LOG2E / (blur * width)
    sqy = jnp.zeros((1, cols), jnp.float32)
    for r in range(0, width, LANES):
        some = yg[r:r + LANES, :].astype(jnp.float32)
        sqy = sqy + jnp.sum(some * some, 0, keepdims=True)
    xstep = 2 * LANES if rows % (2 * LANES) == 0 else LANES

    def cost_block(i):
        xb = xg[:, band(i, xstep)]
        xw = xb.astype(jnp.float32)
        sqx = jnp.sum(xw * xw, 0, keepdims=True)
        sqx = jnp.concatenate([spread(sqx[:, part(k)]) for k in range(xstep // LANES)], 0)
        cross = lax.dot_general(
            xb, yg[...], (((0,), (0,)), ((), ())), preferred_element_type=jnp.float32)
        neg[band(i, xstep), :] = (2.0 * cross - (sqx[:, 0:1] + sqy)) * scale
    each(rows // xstep, cost_block)

    def exchange(slots, count, me, sends, recvs, device):
        def copy(dest, origin):
            return remote(
                slots.at[origin], slots.at[origin], sends.at[dest], recvs.at[origin],
                device(dest))
        others(count, me, lambda p: copy(p, me).start())

        def arrive():
            others(count, me, lambda p: copy(p, p).wait_recv())

        def leave():
            others(count, me, lambda p: copy(p, me).wait_send())
        return arrive, leave

    leaves = []

    def over_cube(t):
        arrive, leave = exchange(fslots.at[t], ncube, q, fs.at[t], fr.at[t], cube_device)
        leaves.append(leave)
        arrive()
        return fslots[t, :, 0:rblocks, :]

    def over_side(t):
        arrive, leave = exchange(gslots.at[t], nside, side, gs.at[t], gr.at[t], side_device)
        leaves.append(leave)
        arrive()
        return gslots[t, :, 0:cblocks, :]

    def set_rows(value):
        fv[0:rblocks, :] = value
        for i in range(rblocks):
            fbc[part(i), :] = spread(fv[i:i + 1, :])

    def first_rows(i):
        here = band(i, LANES)
        high = neg[here, part(0)]
        for k in range(1, cblocks):
            high = jnp.maximum(high, neg[here, part(k)])
        top = jnp.max(high, 1, keepdims=True)
        total = jnp.exp2(neg[here, part(0)] - top)
        for k in range(1, cblocks):
            total = total + jnp.exp2(neg[here, part(k)] - top)
        line = top + jnp.log(jnp.sum(total, 1, keepdims=True)) * LOG2E
        fslots[0, q, pl.ds(i, 1), :] = gather_line(line)
    each(rblocks, first_rows)
    set_rows(log_a - lse2(over_cube(0)))

    def first_cols(k):
        here = band(k, LANES)

        def score(i):
            return neg[part(i), here] + fbc[part(i), :]

        high = score(0)
        for i in range(1, rblocks):
            high = jnp.maximum(high, score(i))
        top = jnp.max(high, 0, keepdims=True)
        total = jnp.exp2(score(0) - top)
        for i in range(1, rblocks):
            total = total + jnp.exp2(score(i) - top)
        line = top + jnp.log(jnp.sum(total, 0, keepdims=True)) * LOG2E
        gslots[0, side, pl.ds(k, 1), :] = line
    each(cblocks, first_cols)
    gv[0:cblocks, :] = log_b - lse2(over_side(0))
    mass_b = b_ref[zl]

    for t in range(1, ITERS):
        for i in range(rblocks):
            total = jnp.zeros((LANES, LANES), jnp.float32)
            for k in range(cblocks):
                if t == 1:
                    value = jnp.exp2(neg[part(i), part(k)] + fbc[part(i), :] + gv[k:k + 1, :])
                    pm[part(i), part(k)] = value
                    total = total + value
                else:
                    total = total + pm[part(i), part(k)] * gv[k:k + 1, :]
            fslots[t, q, i:i + 1, :] = row_sums(total)
        set_rows(mass_a / jnp.sum(over_cube(t), 0))
        for k in range(cblocks):
            total = pm[part(0), part(k)] * fbc[part(0), :]
            for i in range(1, rblocks):
                total = total + pm[part(i), part(k)] * fbc[part(i), :]
            gslots[t, side, k:k + 1, :] = jnp.sum(total, 0, keepdims=True)
        gv[0:cblocks, :] = mass_b / jnp.sum(over_side(t), 0)

    for i in range(rblocks):
        for k in range(cblocks):
            value = pm[part(i), part(k)] * fbc[part(i), :] * gv[k:k + 1, :]
            plan[part(i), part(k)] = value.astype(jnp.bfloat16)

    step = 2 * LANES if cols % (2 * LANES) == 0 else LANES

    def xsum_block(k):
        here = band(k, step)
        xsend[:, here] = jnp.dot(
            xg[...], plan[:, here], preferred_element_type=jnp.float32).astype(jnp.bfloat16)
    each(cols // step, xsum_block)

    def u_across(layer, dest, origin):
        return remote(
            xsend.at[band(layer * yn + dest, fy), :], xmid.at[layer, origin],
            us.at[layer, dest], um.at[layer, origin], (z * yn + dest, col))

    def u_along(dest, origin):
        return remote(
            xout.at[dest], xrecv.at[origin], uo.at[dest], ur.at[origin], (dest * yn + y, col))

    def u_start(layer):
        others(yn, y, lambda dest: u_across(layer, dest, y).start())
    others(zn, z, u_start)
    u_start(z)

    rstep = 2 * LANES if rows % (2 * LANES) == 0 else LANES

    def pull_block(i):
        here = band(i, rstep)
        psend[:, here] = lax.dot_general(
            yg[...], plan[here, :], (((1,), (1,)), ((), ())),
            preferred_element_type=jnp.float32).astype(jnp.bfloat16)
    each(rows // rstep, pull_block)

    def p_place(index):
        return band(lax.div(index, split), fx), band(lax.rem(index, split), own_rows)

    def p_across(index, dest, origin):
        return remote(
            psend.at[p_place(cube_index(index, dest))], pmid.at[index, origin],
            ps.at[index, dest], pk.at[index, origin], cube_device(cube_index(chip, dest)))

    def p_along(dest, origin):
        return remote(
            pout.at[dest], precv.at[origin], po.at[dest], pr.at[origin],
            cube_device(cube_index(dest, c)))

    def p_start(index):
        others(cores, c, lambda dest: p_across(index, dest, c).start())
    others(nchip, chip, p_start)
    p_start(chip)

    def u_total(layer):
        own = xsend[band(layer * yn + y, fy), :].astype(jnp.float32)
        for d in range(1, yn):
            origin = lax.rem(y + d, yn)
            u_across(layer, origin, origin).wait_recv()
            own = own + xmid[layer, origin].astype(jnp.float32)
        return own.astype(jnp.bfloat16)

    def p_total(index):
        own = psend[p_place(cube_index(index, c))].astype(jnp.float32)
        for d in range(1, cores):
            origin = lax.rem(c + d, cores)
            p_across(index, origin, origin).wait_recv()
            own = own + pmid[index, origin].astype(jnp.float32)
        return own.astype(jnp.bfloat16)

    def u_pass(layer):
        xout[layer] = u_total(layer)
        u_along(layer, z).start()

    def p_pass(index):
        pout[index] = p_total(index)
        p_along(index, chip).start()

    others(nchip, chip, p_pass)
    others(zn, z, u_pass)
    precv[chip] = p_total(chip)

    half = rslots.shape[1] // 2
    for i in range(rblocks):
        total = jnp.zeros((LANES, LANES), jnp.float32)
        moment = jnp.zeros((LANES, LANES), jnp.float32)
        for k in range(cblocks):
            weight = pm[part(i), part(k)] * gv[k:k + 1, :]
            total = total + weight
            moment = moment + weight * neg[part(i), part(k)]
        rslots[q, i:i + 1, :] = row_sums(total)
        rslots[q, half + i:half + i + 1, :] = row_sums(moment)
    arrive, leave = exchange(rslots, ncube, q, rs, rr, cube_device)
    leaves.append(leave)
    xrecv[z] = u_total(z)
    arrive()
    total = jnp.sum(rslots[:, 0:rblocks, :], 0)
    moment = jnp.sum(rslots[:, half:half + rblocks, :], 0)
    reward_ref[...] = moment / total * (blur / LOG2E)
    mass_ref[...] = fv[0:rblocks, :] * total

    others(nchip, chip, lambda p: p_along(p, p).wait_recv())
    summed = precv[0].astype(jnp.float32)
    for p in range(1, nchip):
        summed = summed + precv[p].astype(jnp.float32)
    pulled_ref[...] = summed
    others(zn, z, lambda p: u_along(p, p).wait_recv())
    for p in range(split):
        summed = xrecv[p].astype(jnp.float32)
        for s in range(1, zn // split):
            summed = summed + xrecv[s * split + p].astype(jnp.float32)
        xsum_ref[:, p * cols:(p + 1) * cols] = summed

    others(zn, z, lambda p: y_along(p, z).wait_send())
    others(yn, y, lambda p: y_first(p).wait_send())
    others(zn, z, lambda layer: others(
        yn, y, lambda dest: y_across(layer, dest, y).wait_send()))
    others(nchip, chip, lambda p: x_copy(cube_index(p, c), q).wait_send())
    others(cores, c, lambda p: x_copy(cube_index(chip, p), q).wait_send())
    others(nchip, chip, lambda p: others(
        cores, c, lambda core: x_forward(cube_index(p, c), core).wait_send()))
    others(split, zl, lambda p: w_copy(p, zl).wait_send())
    for leave in leaves:
        leave()
    each(zn, lambda layer: others(
        yn, y, lambda dest: u_across(layer, dest, y).wait_send()))
    others(zn, z, lambda p: u_along(p, z).wait_send())
    each(nchip, lambda p: others(
        cores, c, lambda dest: p_across(p, dest, c).wait_send()))
    others(nchip, chip, lambda p: p_along(p, chip).wait_send())


def shards(zn, yn, cn, split, roll_embed, expert_embed, roll_weight, expert_weight):
    fx, own_rows = roll_embed.shape
    fy, own_cols = expert_embed.shape
    width = fx * cn
    rows, cols = own_rows * split, own_cols // split
    rblocks, cblocks = rows // LANES, cols // LANES
    nrow, ncube, nside = zn * yn, cn * split, (zn // split) * yn
    cores = 2 if cn % 2 == 0 else 1
    nchip = ncube // cores
    f32, bf16 = jnp.float32, jnp.bfloat16
    dma = pltpu.SemaphoreType.DMA
    rt, ct, wt = tile_rows(rblocks), tile_rows(cblocks), tile_rows(own_rows // LANES)
    vmem = pl.BlockSpec(memory_space=pltpu.VMEM)
    reward, mass, pulled, xsum = pl.pallas_call(
        functools.partial(kernel, zn, yn, cn, split),
        out_shape=(
            jax.ShapeDtypeStruct((rblocks, LANES), f32),
            jax.ShapeDtypeStruct((rblocks, LANES), f32),
            jax.ShapeDtypeStruct((fx, own_rows), f32),
            jax.ShapeDtypeStruct((fy, own_cols), f32),
        ),
        in_specs=[vmem] * 4,
        out_specs=[vmem] * 4,
        scratch_shapes=[
            pltpu.VMEM((width, rows), bf16),
            pltpu.VMEM((width, cols), bf16),
            pltpu.VMEM((rows, cols), f32),
            pltpu.VMEM((rows, cols), f32),
            pltpu.VMEM((rows, cols), bf16),
            pltpu.VMEM((rows, LANES), f32),
            pltpu.VMEM((split, wt, LANES), f32),
            pltpu.VMEM((ITERS, ncube, rt, LANES), f32),
            pltpu.VMEM((ITERS, nside, ct, LANES), f32),
            pltpu.VMEM((ncube, 2 * rt, LANES), f32),
            pltpu.VMEM((rt, LANES), f32),
            pltpu.VMEM((ct, LANES), f32),
            pltpu.VMEM((width, cols), bf16),
            pltpu.VMEM((zn, yn, fy, cols), bf16),
            pltpu.VMEM((zn, fy, cols), bf16),
            pltpu.VMEM((zn, fy, cols), bf16),
            pltpu.VMEM((width, rows), bf16),
            pltpu.VMEM((nchip, cores, fx, own_rows), bf16),
            pltpu.VMEM((nchip, fx, own_rows), bf16),
            pltpu.VMEM((nchip, fx, own_rows), bf16),
            dma((2,)),
            dma((ncube,)), dma((ncube,)), dma((ncube, cores)),
            dma((zn,)), dma((nrow,)), dma((zn, yn)),
            dma((split,)), dma((split,)),
            dma((ITERS, ncube)), dma((ITERS, ncube)),
            dma((ITERS, nside)), dma((ITERS, nside)),
            dma((ncube,)), dma((ncube,)),
            dma((zn, yn)), dma((zn, yn)), dma((zn,)), dma((zn,)),
            dma((nchip, cores)), dma((nchip, cores)), dma((nchip,)), dma((nchip,)),
        ],
        compiler_params=pltpu.CompilerParams(
            collective_id=0, has_side_effects=True, vmem_limit_bytes=48 * 2**20),
        cost_estimate=pl.CostEstimate(
            flops=6 * rows * cols * width, bytes_accessed=4 * fy * own_cols,
            transcendentals=3 * rows * cols),
    )(
        roll_embed, expert_embed,
        roll_weight.reshape(own_rows // LANES, LANES),
        expert_weight.reshape(split, cblocks, LANES),
    )
    start = lax.rem(lax.div(lax.axis_index("row"), yn), split) * own_rows
    reward = lax.dynamic_slice_in_dim(reward.reshape(rows), start, own_rows, 0)
    mass = lax.dynamic_slice_in_dim(mass.reshape(rows), start, own_rows, 0)
    roll_pull = mass[None, :] * roll_embed.astype(f32) - pulled
    expert_pull = expert_weight[None, :] * expert_embed.astype(f32) - xsum
    return (reward, roll_pull, expert_pull)


def solution(mesh):
    cn = mesh.shape["col"]
    yn = max(cn // 2, 1)
    if mesh.shape["row"] % yn:
        yn = 1
    zn = mesh.shape["row"] // yn
    split = 2 if zn % 2 == 0 else 1
    placed = (P("col", "row"), P("row", "col"), P("row"), P("col"))
    return jax.shard_map(
        functools.partial(shards, zn, yn, cn, split),
        mesh=mesh,
        in_specs=placed,
        out_specs=(P("row"), P("col", "row"), P("row", "col")),
        check_vma=False,
    )
```
